32 devices in a mesh: expert: 4 (over z), etp: 2 (over x), tp: 4 (over y, core).
Axes of the slice: x: 2, y: 2, z: 4, core: 2. Of those that a mesh axis runs over, the one named last changes fastest.
Arguments:
- d_out: bfloat16 [2048, 6144], P(('expert', 'tp'), 'etp'), may hold values from -6 to 6
- expert_ids: int32 [2048, 2], P(('expert', 'tp')), may hold values from 0 to 3, all different within a row; in each aligned block of 128 rows (0 to 127, 128 to 255, ...) at most 64 rows name the same one
- gate_weights: float32 [2048, 2], P(('expert', 'tp')), may hold values from 0.05 to 0.95, as said below
- saved_gate: bfloat16 [4, 1024, 16384], P('expert', None, ('etp', 'tp')), may hold values from -8 to 8
- saved_up: bfloat16 [4, 1024, 16384], P('expert', None, ('etp', 'tp')), may hold values from -6 to 6
- w_gate: bfloat16 [4, 6144, 16384], P('expert', None, ('etp', 'tp')), may hold values from -0.078125 to 0.078125
- w_up: bfloat16 [4, 6144, 16384], P('expert', None, ('etp', 'tp')), may hold values from -0.078125 to 0.078125
- w_down: bfloat16 [4, 16384, 6144], P('expert', ('etp', 'tp')), may hold values from -0.046875 to 0.046875
- w_out: bfloat16 [6144, 6144], P('tp', 'etp'), may hold values from -0.078125 to 0.078125
Outputs:
- d_hidden: bfloat16 [2048, 6144], P(('expert', 'tp'), 'etp')
- d_heads: bfloat16 [2048, 6144], P(('expert', 'etp'), 'tp')
The draws below stay inside these ranges and needn't reach their ends.
Inputs may be any that keep to these rules, and one draw needn't show every extreme that they name: `expert_ids`: each token names two different experts; in every block of 128 tokens every expert is named by exactly 64 tokens. `gate_weights`: a token's two weights sum to one.
All inputs are finite; a program needn't handle non-finite values.
Results may differ from the reference program's by a relative error of at most 0.02.
Values may be sent and summed in bfloat16 or wider, within the bound.
A program may use at most 192 MiB of HBM per device.

```python
import math
import jax
import jax.numpy as jnp
import numpy as np
from jax import lax

D = 6144
FF = 16384
TOK_GRP = 128
EXPERTS = 4
HD = 6144
CAP = 64
TOKENS = 2048
ROWS = 1024
N_EXPERT = 4
N_ETP = 2
N_TP = 4


def draw_gate_weights(key, part):
    first_weight = jax.random.uniform(key, (TOKENS, 1), jnp.float32, 0.2, 0.8)
    return jnp.concatenate([first_weight, 1.0 - first_weight], axis=1)


def block_levels(own_key, dims, cuts, least, largest):
    gain = 1.0
    for axis_at, shards_of in cuts:
        heights = jax.random.uniform(jax.random.fold_in(jax.random.fold_in(own_key, 6), axis_at), (shards_of,), jnp.float32, least / len(cuts), largest / len(cuts))
        gain = gain * jnp.repeat(jnp.exp(heights), dims[axis_at] // shards_of).reshape((-1,) + (1,) * (len(dims) - 1 - axis_at))
    return gain


def assign_block(rng, own, number, rows, count, top, reach, lean):
    order = jax.random.permutation(rng, count)
    crowded, common = load_shares(count, rows * top, reach, lean, True), load_shares(count, rows * top, reach, lean, False)
    places = jnp.arange(count)

    def named(lengths, rotation):
        used = int((lengths > 0).sum())
        fixed = max(1, used // 4)
        passed = fixed + (places - fixed + rotation * (used - fixed)) % max(1, count - fixed)
        return jnp.zeros((count,), jnp.int32).at[order[jnp.where(places < fixed, places, passed)]].set(jnp.asarray(lengths, jnp.int32))

    lengths = jnp.where(number % 4 == 0, named(crowded, number // 4), named(common, number - number // 4 - 1))
    mixed = jax.random.permutation(jax.random.fold_in(own, 3), count)
    donor, receiver = mixed[0:count // 2 * 2:2], mixed[1:count // 2 * 2:2]
    slack = jnp.minimum(lengths[donor] - 1, reach - lengths[receiver]) // 2
    slack = jnp.where((donor == order[0]) | (receiver == order[0]) | (lengths[receiver] == 0), 0, jnp.maximum(slack, 0))
    passed = jax.random.randint(jax.random.fold_in(own, 4), (count // 2,), 0, 1 << 20) % (slack + 1)
    lengths = lengths.at[donor].add(-passed).at[receiver].add(passed)
    labels = jnp.searchsorted(jnp.cumsum(lengths), jnp.arange(rows * top), side="right").astype(jnp.int32)
    listing = labels.reshape(top, rows).T
    listing = listing[jax.random.permutation(jax.random.fold_in(own, 1), rows)]
    rotation = jax.random.randint(jax.random.fold_in(own, 2), (rows, 1), 0, top)
    return jnp.take_along_axis(listing, (jnp.arange(top)[None, :] + rotation) % top, axis=1)


def load_shares(count, total, bound, slope, full):
    portions = [(1 << 20) // math.isqrt(standing ** slope) + 1 for standing in range(1, count + 1)]
    largest = bound if full else min(bound, max(-(-total // count), total * portions[0] // sum(portions)))
    least = 1 if total - largest >= count - 1 else 0
    counts, spare = [largest] + [least] * (count - 1), total - largest - least * (count - 1)
    while spare > 0:
        candidates = [i for i in range(1, count) if counts[i] < largest] or [i for i in range(1, count) if counts[i] < bound]
        pool, budget = sum([portions[i] for i in candidates]), spare
        for i in candidates:
            extra = min(bound - counts[i], max(1, budget * portions[i] // pool), spare)
            counts[i] = counts[i] + extra
            spare = spare - extra
    return np.array(counts)


def scatter_about(own_key, dims, width, reach, pieces=(), kind=jnp.bfloat16):
    drawn = width * jax.random.normal(own_key, dims, jnp.float32)
    if pieces:
        drawn = drawn * block_levels(own_key, dims, pieces, -0.22, 0.18)
    return jnp.clip(drawn, -reach, reach).astype(kind)


def setup_inputs(seed: int = 0) -> dict:
    key_of = jax.random.split(jax.random.key(seed), 10)
    d_out = scatter_about(key_of[0], (TOKENS, D), 1.0, 6.0, ((0, 16), (1, 2)))
    expert_ids_keys = jax.random.split(jax.random.fold_in(key_of[1], 1), TOKENS // TOK_GRP)
    expert_ids_turns = jax.random.permutation(jax.random.fold_in(key_of[1], 3), TOKENS // TOK_GRP)
    expert_ids = jax.vmap(lambda own, number: assign_block(jax.random.fold_in(key_of[1], 2), own, number, TOK_GRP, EXPERTS, 2, CAP, 0))(expert_ids_keys, expert_ids_turns).reshape((TOKENS, 2))
    gate_weights = draw_gate_weights(jax.random.fold_in(key_of[9], 71), 0)
    saved_gate = scatter_about(key_of[3], (EXPERTS, ROWS, FF), 2.0, 8.0, ((0, 4), (2, 8)))
    saved_up = scatter_about(key_of[4], (EXPERTS, ROWS, FF), 1.0, 6.0, ((0, 4), (2, 8)))
    w_gate = scatter_about(key_of[5], (EXPERTS, D, FF), D ** -0.5, 0.078125, ((0, 4), (2, 8)))
    w_up = scatter_about(key_of[6], (EXPERTS, D, FF), D ** -0.5, 0.078125, ((0, 4), (2, 8)))
    w_down = scatter_about(key_of[7], (EXPERTS, FF, D), FF ** -0.5, 0.046875, ((0, 4), (1, 8)))
    w_out = scatter_about(key_of[8], (HD, D), HD ** -0.5, 0.078125, ((0, 4), (1, 2)))
    return {"d_out": d_out, "expert_ids": expert_ids, "gate_weights": gate_weights, "saved_gate": saved_gate, "saved_up": saved_up, "w_gate": w_gate, "w_up": w_up, "w_down": w_down, "w_out": w_out}


def expert_backward(rows_in, gate_saved, up_saved, gate_matrix, up_matrix, down_matrix):
    grad_act = jnp.dot(rows_in, down_matrix.T, preferred_element_type=jnp.float32)
    gate_val = gate_saved.astype(jnp.float32)
    up_val = up_saved.astype(jnp.float32)
    sigma = jax.nn.sigmoid(gate_val)
    grad_up = (grad_act * gate_val * sigma).astype(jnp.bfloat16)
    grad_gate = (grad_act * up_val * sigma * (1.0 + gate_val * (1.0 - sigma))).astype(jnp.bfloat16)
    run_count = N_ETP * N_TP
    run_len = FF // run_count

    def add_run(index, total):
        start = (index * run_len).astype(jnp.int32)
        gate_piece = lax.dynamic_slice_in_dim(grad_gate, start, run_len, 1)
        up_piece = lax.dynamic_slice_in_dim(grad_up, start, run_len, 1)
        gate_cols = lax.dynamic_slice_in_dim(gate_matrix, start, run_len, 1)
        up_cols = lax.dynamic_slice_in_dim(up_matrix, start, run_len, 1)
        first_part = jnp.dot(gate_piece, gate_cols.T, preferred_element_type=jnp.float32)
        partial_sum = first_part + jnp.dot(up_piece, up_cols.T, preferred_element_type=jnp.float32)
        return total + partial_sum.astype(jnp.bfloat16).astype(jnp.float32)

    initial = jnp.zeros((rows_in.shape[0], gate_matrix.shape[0]), jnp.float32)
    return lax.fori_loop(0, run_count, add_run, initial)


def reference(d_out, expert_ids, gate_weights, saved_gate, saved_up, w_gate, w_up, w_down, w_out):
    owners = N_EXPERT * N_TP
    experts_iota = jnp.arange(EXPERTS, dtype=jnp.int32)
    first_hit = (expert_ids[:, 0:1] == experts_iota[None, :])
    second_hit = (expert_ids[:, 1:2] == experts_iota[None, :])
    member = first_hit.astype(jnp.int32) + second_hit.astype(jnp.int32)
    weight = gate_weights[:, 0:1] * first_hit.astype(jnp.float32) + gate_weights[:, 1:2] * second_hit.astype(jnp.float32)
    member_blk = member.reshape(owners, TOK_GRP, EXPERTS)
    slot = jnp.cumsum(member_blk, axis=1) - member_blk
    slot_iota = jnp.arange(CAP, dtype=jnp.int32)
    select = ((slot[:, :, :, None] == slot_iota[None, None, None, :]) & (member_blk[:, :, :, None] > 0)).astype(jnp.float32)
    weighted_sel = select * weight.reshape(owners, TOK_GRP, EXPERTS)[:, :, :, None]
    grads_blk = d_out.reshape(owners, TOK_GRP, D).astype(jnp.float32)
    dispatched = jnp.einsum("otec,otd->eocd", weighted_sel, grads_blk, precision=lax.Precision.HIGHEST).astype(jnp.bfloat16)
    returned_all = []
    for expert in range(EXPERTS):
        rows_in = dispatched[expert].reshape(owners * CAP, D)
        result = expert_backward(rows_in, saved_gate[expert], saved_up[expert], w_gate[expert], w_up[expert], w_down[expert])
        returned_all.append(result.reshape(owners, CAP, D))
    returned = jnp.stack(returned_all, axis=0)
    d_moe = jnp.einsum("otec,eocd->otd", select, returned, precision=lax.Precision.HIGHEST).reshape(TOKENS, D)
    d_hidden = (d_out.astype(jnp.float32) + d_moe).astype(jnp.bfloat16)
    feat_run = D // N_ETP
    head_total = jnp.zeros((TOKENS, HD), jnp.float32)
    for run in range(N_ETP):
        hidden_piece = d_hidden[:, run * feat_run:(run + 1) * feat_run]
        out_piece = w_out[:, run * feat_run:(run + 1) * feat_run]
        head_piece = jnp.dot(hidden_piece, out_piece.T, preferred_element_type=jnp.float32)
        head_total = head_total + head_piece.astype(jnp.bfloat16).astype(jnp.float32)
    d_heads = head_total.astype(jnp.bfloat16)
    return d_hidden, d_heads
```

```python
import functools

import jax
import jax.numpy as jnp
from jax import lax
from jax.experimental import pallas as pl
from jax.experimental.pallas import tpu as pltpu
from jax.sharding import PartitionSpec as P

NT = (((1,), (1,)), ((), ()))
TILE = 256
COLUMN_PARTS = 4


def act_kernel(cap, width, aliased, s_ref, *refs):
    own0, own1, own2, own3, oth0, oth1, lo2, hi2, lo3, hi3, wd, sg, su = refs[:13]
    gg, gu, lhs = refs[-3:]

    @pl.when(pl.program_id(0) == 0)
    def _():
        mine = pl.ds(pl.multiple_of(s_ref[0], 128), width)
        other = pl.ds(pl.multiple_of(s_ref[1], 128), width)
        for r, block in enumerate((own0, own1, own2, own3)):
            lhs[r * cap:(r + 1) * cap, mine] = block[...]
        for r, block in enumerate((oth0, oth1)):
            lhs[r * cap:(r + 1) * cap, other] = block[...]
        half = cap // 2
        for r, (low, high) in ((2, (lo2, hi2)), (3, (lo3, hi3))):
            lhs[r * cap:r * cap + half, other] = low[...]
            lhs[r * cap + half:(r + 1) * cap, other] = high[...]

    acc = lax.dot_general(lhs[...], wd[...], NT, preferred_element_type=jnp.float32)
    for r in range(4):
        rows = pl.ds(pl.multiple_of(s_ref[3 + r], cap), cap)
        here = slice(r * cap, (r + 1) * cap)
        g = sg[rows, :].astype(jnp.float32)
        u = su[rows, :].astype(jnp.float32)
        s = 1.0 / (1.0 + jnp.exp(-g))
        d = acc[here, :] * s
        gu[here, :] = (d * g).astype(jnp.bfloat16)
        gg[here, :] = (d * u * (1.0 + g * (1.0 - s))).astype(jnp.bfloat16)


def act_call(k, scalars, blocks, w_down, saved_gate, saved_up, sofar):
    cap, width = blocks[0].shape
    rows_all, hidden = saved_gate.shape[1:]
    model = w_down.shape[2]
    rows = 4 * cap
    full = [pl.BlockSpec(b.shape, lambda n, s: (0, 0)) for b in blocks]
    wide = pl.BlockSpec((None, TILE, model), lambda n, s: (0, n, 0))
    saved = pl.BlockSpec((None, rows, TILE), lambda n, s: (0, s[2], n))
    held = [pl.BlockSpec(memory_space=pl.ANY)] * len(sofar)
    out = pl.BlockSpec((rows, TILE), lambda n, s: (k, n))
    count = 1 + len(blocks) + 3
    return pl.pallas_call(
        functools.partial(act_kernel, cap, width, len(sofar)),
        out_shape=[jax.ShapeDtypeStruct((rows_all, hidden), jnp.bfloat16)] * 2,
        grid_spec=pltpu.PrefetchScalarGridSpec(
            num_scalar_prefetch=1,
            grid=(hidden // TILE,),
            in_specs=full + [wide, saved, saved] + held,
            out_specs=[out, out],
            scratch_shapes=[pltpu.VMEM((rows, model), jnp.bfloat16)],
        ),
        input_output_aliases={count + i: i for i in range(len(sofar))},
        compiler_params=pltpu.CompilerParams(vmem_limit_bytes=50 * 2**20),
        cost_estimate=pl.CostEstimate(
            flops=2 * rows * model * hidden,
            bytes_accessed=2 * (hidden * model + rows * model + 4 * rows * hidden),
            transcendentals=rows * hidden,
        ),
        name="act",
    )(scalars, *blocks, w_down, saved_gate, saved_up, *sofar)


def grad_kernel(cap, experts, s_ref, gg, gu, wg, wu, keep, send):
    res = lax.dot_general(gg[...], wg[...], NT, preferred_element_type=jnp.float32)
    res += lax.dot_general(gu[...], wu[...], NT, preferred_element_type=jnp.float32)
    res = res.astype(jnp.bfloat16)
    for k in range(experts):
        for v in range(2):
            at = (4 * k + 2 * v) * cap
            keep[v, k * cap:(k + 1) * cap, :] = res[at:at + cap]
            send[v, k * cap:(k + 1) * cap, :] = res[at + cap:at + 2 * cap]


def grad_call(part, columns, starts, gg, gu, w_gate, w_up, cap):
    rows_all, hidden = gg.shape
    experts = rows_all // (4 * cap)
    lhs = pl.BlockSpec((rows_all, hidden), lambda h, n, s: (0, 0))
    first = part * (columns // TILE)
    wide = pl.BlockSpec((None, TILE, hidden), lambda h, n, s: (0, s[h] + first + n, 0))
    out = pl.BlockSpec((None, 2, experts * cap, TILE), lambda h, n, s: (h, 0, 0, n))
    return pl.pallas_call(
        functools.partial(grad_kernel, cap, experts),
        out_shape=[jax.ShapeDtypeStruct((2, 2, experts * cap, columns), jnp.bfloat16)] * 2,
        grid_spec=pltpu.PrefetchScalarGridSpec(
            num_scalar_prefetch=1,
            grid=(2, columns // TILE),
            in_specs=[lhs, lhs, wide, wide],
            out_specs=[out, out],
        ),
        compiler_params=pltpu.CompilerParams(vmem_limit_bytes=50 * 2**20),
        cost_estimate=pl.CostEstimate(
            flops=8 * rows_all * hidden * columns,
            bytes_accessed=2 * (2 * rows_all * hidden + 4 * hidden * columns + 2 * rows_all * columns),
            transcendentals=0,
        ),
        name="grad",
    )(starts, gg, gu, w_gate, w_up)


def planned(d_out, expert_ids, gate_weights, saved_gate, saved_up, w_gate, w_up, w_down, w_out):
    f32, bf16 = jnp.float32, jnp.bfloat16
    experts = lax.axis_size("expert")
    z, x, t = lax.axis_index("expert"), lax.axis_index("etp"), lax.axis_index("tp")
    y, c = t // 2, t % 2
    tokens, width = d_out.shape
    cap = saved_gate.shape[1] // (experts * 4)

    def over_z(v, shift):
        if shift % experts == 0:
            return v
        return lax.ppermute(v, "expert", [(i, (i + shift) % experts) for i in range(experts)])

    def over_x(v):
        return lax.ppermute(v, "etp", [(0, 1), (1, 0)])

    def over_y(v):
        return lax.ppermute(v, "tp", [(i, i ^ 2) for i in range(4)])

    def over_core(v):
        return lax.ppermute(v, "tp", [(i, i ^ 1) for i in range(4)])

    names = (z + jnp.arange(experts, dtype=jnp.int32)) % experts
    first_hit = expert_ids[:, 0:1] == names[None, :]
    second_hit = expert_ids[:, 1:2] == names[None, :]
    member = first_hit.astype(jnp.int32) + second_hit.astype(jnp.int32)
    weight = gate_weights[:, 0:1] * first_hit.astype(f32) + gate_weights[:, 1:2] * second_hit.astype(f32)
    slot = jnp.cumsum(member, axis=0) - member
    slot_iota = jnp.arange(cap, dtype=jnp.int32)
    select = (slot[:, :, None] == slot_iota[None, None, :]) & (member[:, :, None] > 0)
    slot_weight = jnp.sum(jnp.where(select, weight[:, :, None], 0.0), axis=0)
    select = select.astype(bf16)

    gathered = []
    for k in range(experts):
        rows = lax.dot_general(
            select[:, k], d_out, (((0,), (0,)), ((), ())), preferred_element_type=f32
        )
        gathered.append(over_z((rows * slot_weight[k][:, None]).astype(bf16), k))

    grads = ()
    half = cap // 2
    for k in range(experts):
        a = gathered[k]
        bx, by = over_x(a), over_y(a)
        low, high = over_y(bx[:half]), over_x(by[half:])
        blocks = (
            a, over_core(a), by, over_core(by),
            bx, over_core(bx), low, high, over_core(low), over_core(high),
        )
        scalars = jnp.stack(
            [x * width, (1 - x) * width, (z - k) % experts] + [(t ^ r) * cap for r in range(4)]
        ).astype(jnp.int32)
        grads = act_call(k, scalars, blocks, w_down, saved_gate, saved_up, grads)
    gg, gu = grads

    columns = width // COLUMN_PARTS
    starts = jnp.stack([x, 1 - x]).astype(jnp.int32) * (width // TILE)
    cut = experts // 2 * cap
    hidden_parts, head_rows = [], []
    for part in range(COLUMN_PARTS):
        keep, send = grad_call(part, columns, starts, gg, gu, w_gate, w_up, cap)
        both = (keep.astype(f32) + over_core(send).astype(f32)).astype(bf16)
        via_x, via_y = over_x(both[1, 1, :cut]), over_y(both[1, 1, cut:])
        to_y = jnp.concatenate(
            [(both[0, 1, :cut].astype(f32) + via_x.astype(f32)).astype(bf16), both[0, 1, cut:]]
        )
        to_x = jnp.concatenate(
            [both[1, 0, :cut], (both[1, 0, cut:].astype(f32) + via_y.astype(f32)).astype(bf16)]
        )
        from_x, from_y = over_x(to_x), over_y(to_y)
        own = (both[0, 0].astype(f32) + from_x.astype(f32) + from_y.astype(f32)).astype(bf16)
        back = [over_z(own[k * cap:(k + 1) * cap], -k) for k in range(experts)]
        d_moe = 0.0
        for k in range(experts):
            d_moe = d_moe + jnp.dot(select[:, k], back[k], preferred_element_type=f32)
        here = d_out[:, part * columns:(part + 1) * columns].astype(f32)
        piece = (here + d_moe).astype(bf16)
        hidden_parts.append(piece)
        across = over_y(piece)
        head_rows.append(
            jnp.concatenate([piece, over_core(piece), across, over_core(across)], axis=0)
        )
    d_hidden = jnp.concatenate(hidden_parts, axis=1)
    head = 0.0
    for part in range(COLUMN_PARTS):
        head = head + lax.dot_general(
            head_rows[part],
            w_out[:, part * columns:(part + 1) * columns],
            NT,
            preferred_element_type=f32,
        )
    head = head.astype(bf16).reshape(2, 2 * tokens, w_out.shape[0])
    mine = jnp.where(y == x, head[0], head[1])
    theirs = jnp.where(y == x, head[1], head[0])
    total = (mine.astype(f32) + over_x(theirs).astype(f32)).astype(bf16)
    swapped = jnp.concatenate([total[tokens:], total[:tokens]], axis=0)
    return d_hidden, jnp.where(c == 0, total, swapped)


def general(d_out, expert_ids, gate_weights, saved_gate, saved_up, w_gate, w_up, w_down, w_out):
    expert_count = lax.axis_size("expert")
    tp_count = lax.axis_size("tp")
    feat_local = d_out.shape[1]
    cap_slots = saved_gate.shape[1] // (expert_count * tp_count)
    model_width = w_gate.shape[1]
    experts_iota = jnp.arange(expert_count, dtype=jnp.int32)
    first_hit = expert_ids[:, 0:1] == experts_iota[None, :]
    second_hit = expert_ids[:, 1:2] == experts_iota[None, :]
    member = first_hit.astype(jnp.int32) + second_hit.astype(jnp.int32)
    weight = gate_weights[:, 0:1] * first_hit.astype(jnp.float32) + gate_weights[
        :, 1:2
    ] * second_hit.astype(jnp.float32)
    slot = jnp.cumsum(member, axis=0) - member
    slot_iota = jnp.arange(cap_slots, dtype=jnp.int32)
    select = ((slot[:, :, None] == slot_iota[None, None, :]) & (member[:, :, None] > 0)).astype(
        jnp.float32
    )
    weighted_sel = select * weight[:, :, None]
    outgoing = jnp.einsum(
        "tec,td->ecd", weighted_sel, d_out.astype(jnp.float32), precision=lax.Precision.HIGHEST
    ).astype(jnp.bfloat16)
    received = lax.all_to_all(outgoing, "expert", split_axis=0, concat_axis=0, tiled=True)
    blocks_all = lax.all_gather(received[:, None], "tp", axis=1, tiled=True)
    down_local = w_down[0]
    slot_rows = blocks_all.shape[0] * blocks_all.shape[1] * blocks_all.shape[2]
    shard_piece = lax.all_gather(blocks_all, "etp", axis=3, tiled=True)
    width_piece = shard_piece.shape[3]
    flat_rows = shard_piece.reshape(slot_rows, width_piece)
    grad_act = lax.dot_general(
        flat_rows, down_local, (((1,), (1,)), ((), ())), preferred_element_type=jnp.float32
    )
    gate_val = saved_gate[0].astype(jnp.float32)
    up_val = saved_up[0].astype(jnp.float32)
    sigma = jax.nn.sigmoid(gate_val)
    grad_up = (grad_act * gate_val * sigma).astype(jnp.bfloat16)
    grad_gate = (grad_act * up_val * sigma * (1.0 + gate_val * (1.0 - sigma))).astype(jnp.bfloat16)
    gate_local = w_gate[0]
    up_local = w_up[0]
    first_part = lax.dot_general(
        gate_local, grad_gate, (((1,), (1,)), ((), ())), preferred_element_type=jnp.float32
    )
    whole_term = (
        first_part
        + lax.dot_general(
            up_local, grad_up, (((1,), (1,)), ((), ())), preferred_element_type=jnp.float32
        )
    ).reshape(model_width, expert_count, tp_count, cap_slots)
    by_block = lax.psum_scatter(
        whole_term.astype(jnp.bfloat16), "tp", scatter_dimension=2, tiled=True
    )
    reduced = lax.psum_scatter(by_block, "etp", scatter_dimension=0, tiled=True).astype(jnp.float32)
    returned = lax.all_to_all(
        reduced.reshape(feat_local, expert_count, cap_slots).astype(jnp.bfloat16),
        "expert",
        split_axis=1,
        concat_axis=1,
        tiled=True,
    ).astype(jnp.float32)
    d_moe = jnp.einsum("tec,dec->td", select, returned, precision=lax.Precision.HIGHEST)
    d_hidden = (d_out.astype(jnp.float32) + d_moe).astype(jnp.bfloat16)
    head_partial = lax.dot_general(
        lax.all_gather(d_hidden, "tp", axis=0, tiled=True),
        w_out,
        (((1,), (1,)), ((), ())),
        preferred_element_type=jnp.float32,
    )
    d_heads = lax.psum_scatter(
        head_partial.astype(jnp.bfloat16), "etp", scatter_dimension=0, tiled=True
    )
    return (d_hidden, d_heads)


def solution(mesh):
    pair_of_pairs = mesh.shape["etp"] == 2 and mesh.shape["tp"] == 4
    body = planned if pair_of_pairs else general
    in_specs = (
        P(("expert", "tp"), "etp"),
        P(("expert", "tp"), None),
        P(("expert", "tp"), None),
        P("expert", None, ("etp", "tp")),
        P("expert", None, ("etp", "tp")),
        P("expert", None, ("etp", "tp")),
        P("expert", None, ("etp", "tp")),
        P("expert", ("etp", "tp"), None),
        P("tp", "etp"),
    )
    out_specs = (P(("expert", "tp"), "etp"), P(("expert", "etp"), "tp"))
    return jax.shard_map(body, mesh=mesh, in_specs=in_specs, out_specs=out_specs, check_vma=False)
```

```python
import functools

import jax
import jax.numpy as jnp
from jax import lax
from jax.experimental import pallas as pl
from jax.experimental.pallas import tpu as pltpu
from jax.sharding import PartitionSpec as P

NT = (((1,), (1,)), ((), ()))
TILE = 256
COLUMN_PARTS = 4


def send_kernel(sel, rows, scale, *refs):
    out = refs[-1]
    picked = jnp.dot(sel[...], rows[...], preferred_element_type=jnp.float32)
    out[...] = (picked * scale[...]).astype(jnp.bfloat16)


def send_call(sel, rows, scale, after):
    whole = pl.BlockSpec(memory_space=pltpu.VMEM)
    shape = (sel.shape[0], rows.shape[1])
    return pl.pallas_call(
        send_kernel,
        out_shape=jax.ShapeDtypeStruct(shape, jnp.bfloat16),
        in_specs=[whole] * 3 + [pl.BlockSpec(memory_space=pl.ANY)] * len(after),
        out_specs=whole,
        cost_estimate=pl.CostEstimate(
            flops=2 * sel.shape[0] * rows.size,
            bytes_accessed=2 * (rows.size + shape[0] * shape[1]),
            transcendentals=0,
        ),
        name="dispatch",
    )(sel, rows, scale, *after)


def act_kernel(cap, width, groups, s_ref, *refs):
    blocks = refs[:10 * groups]
    wd = refs[10 * groups]
    saved = refs[10 * groups + 1:12 * groups + 1]
    gg, gu, lhs = refs[-3:]

    @pl.when(pl.program_id(0) == 0)
    def _():
        mine = pl.ds(pl.multiple_of(s_ref[0], 128), width)
        other = pl.ds(pl.multiple_of(s_ref[1], 128), width)
        half = cap // 2
        for j in range(groups):
            own0, own1, own2, own3, oth0, oth1, lo2, hi2, lo3, hi3 = blocks[10 * j:10 * j + 10]
            base = 4 * cap * j
            for r, block in enumerate((own0, own1, own2, own3)):
                lhs[base + r * cap:base + (r + 1) * cap, mine] = block[...]
            for r, block in enumerate((oth0, oth1)):
                lhs[base + r * cap:base + (r + 1) * cap, other] = block[...]
            for r, (low, high) in ((2, (lo2, hi2)), (3, (lo3, hi3))):
                lhs[base + r * cap:base + r * cap + half, other] = low[...]
                lhs[base + r * cap + half:base + (r + 1) * cap, other] = high[...]

    acc = lax.dot_general(lhs[...], wd[...], NT, preferred_element_type=jnp.float32)
    for j in range(groups):
        sg, su = saved[2 * j:2 * j + 2]
        for r in range(4):
            rows = pl.ds(pl.multiple_of(s_ref[2 + r], cap), cap)
            here = slice((4 * j + r) * cap, (4 * j + r + 1) * cap)
            g = sg[rows, :].astype(jnp.float32)
            u = su[rows, :].astype(jnp.float32)
            s = 1.0 / (1.0 + jnp.exp(-g))
            d = acc[here, :] * s
            gu[here, :] = (d * g).astype(jnp.bfloat16)
            gg[here, :] = (d * u * (1.0 + g * (1.0 - s))).astype(jnp.bfloat16)


def act_call(at, first, count, scalars, groups, w_down, saved_gate, saved_up, sofar, after):
    cap, width = groups[0][0].shape
    rows_all, hidden = saved_gate.shape[1:]
    model = w_down.shape[2]
    rows = 4 * cap * len(groups)
    blocks = [b for group in groups for b in group]
    full = [pl.BlockSpec(b.shape, lambda n, s: (0, 0)) for b in blocks]
    wide = pl.BlockSpec((None, TILE, model), lambda n, s: (0, first + n, 0))
    saved = []
    for j in range(len(groups)):
        saved += [pl.BlockSpec((None, 4 * cap, TILE), lambda n, s, j=j: (0, s[6 + j], first + n))] * 2
    held = [pl.BlockSpec(memory_space=pl.ANY)] * (len(sofar) + len(after))
    out = pl.BlockSpec((rows, TILE), lambda n, s: (at, first + n))
    ahead = 1 + len(blocks) + 1 + len(saved)
    return pl.pallas_call(
        functools.partial(act_kernel, cap, width, len(groups)),
        out_shape=[jax.ShapeDtypeStruct((rows_all, hidden), jnp.bfloat16)] * 2,
        grid_spec=pltpu.PrefetchScalarGridSpec(
            num_scalar_prefetch=1,
            grid=(count,),
            in_specs=full + [wide] + saved + held,
            out_specs=[out, out],
            scratch_shapes=[pltpu.VMEM((rows, model), jnp.bfloat16)],
        ),
        input_output_aliases={ahead + i: i for i in range(len(sofar))},
        compiler_params=pltpu.CompilerParams(vmem_limit_bytes=50 * 2**20),
        cost_estimate=pl.CostEstimate(
            flops=2 * rows * model * count * TILE,
            bytes_accessed=2 * (count * TILE * model + rows * model + 4 * rows * count * TILE),
            transcendentals=rows * count * TILE,
        ),
        name="act",
    )(scalars, *blocks, w_down, *([saved_gate, saved_up] * len(groups)), *sofar, *after)


def corner_call(bx, by, after):
    half = bx.shape[0] // 2

    def kernel(bx_ref, by_ref, *refs):
        low, high = refs[-2:]
        low[...] = bx_ref[:half]
        high[...] = by_ref[half:]

    whole = pl.BlockSpec(memory_space=pltpu.VMEM)
    return pl.pallas_call(
        kernel,
        out_shape=[jax.ShapeDtypeStruct((half, bx.shape[1]), bx.dtype)] * 2,
        in_specs=[whole] * 2 + [pl.BlockSpec(memory_space=pl.ANY)] * len(after),
        out_specs=[whole] * 2,
        cost_estimate=pl.CostEstimate(flops=0, bytes_accessed=6 * bx.size, transcendentals=0),
        name="corner",
    )(bx, by, *after)


def merge_call(keep, received, other, via_x, via_y, after):
    rows, columns = keep.shape[1:]
    cut = rows // 2

    def kernel(keep_ref, got_ref, other_ref, vx_ref, vy_ref, *refs):
        to_x, to_y, own = refs[-3:]
        f32 = jnp.float32
        own[...] = (keep_ref[0].astype(f32) + got_ref[0].astype(f32)).astype(own.dtype)
        far = keep_ref[1].astype(f32) + got_ref[1].astype(f32)
        to_y[:cut] = (far[:cut] + vx_ref[...].astype(f32)).astype(to_y.dtype)
        to_y[cut:] = far[cut:].astype(to_y.dtype)
        to_x[:cut] = other_ref[0, :cut]
        to_x[cut:] = (other_ref[0, cut:].astype(f32) + vy_ref[...].astype(f32)).astype(to_x.dtype)

    whole = pl.BlockSpec(memory_space=pltpu.VMEM)
    return pl.pallas_call(
        kernel,
        out_shape=[jax.ShapeDtypeStruct((rows, columns), keep.dtype)] * 3,
        in_specs=[whole] * 5 + [pl.BlockSpec(memory_space=pl.ANY)] * len(after),
        out_specs=[whole] * 3,
        cost_estimate=pl.CostEstimate(
            flops=4 * rows * columns, bytes_accessed=20 * rows * columns, transcendentals=0
        ),
        name="merge",
    )(keep, received, other, via_x, via_y, *after)


def grad_kernel(cap, experts, s_ref, gg, gu, wg, wu, *refs):
    keep, send = refs[-2:]
    res = lax.dot_general(gg[...], wg[...], NT, preferred_element_type=jnp.float32)
    res += lax.dot_general(gu[...], wu[...], NT, preferred_element_type=jnp.float32)
    res = res.astype(jnp.bfloat16)
    for k in range(experts):
        for v in range(2):
            at = (4 * k + 2 * v) * cap
            keep[v, k * cap:(k + 1) * cap, :] = res[at:at + cap]
            send[v, k * cap:(k + 1) * cap, :] = res[at + cap:at + 2 * cap]


def grad_call(h, part, columns, starts, gg, gu, w_gate, w_up, cap, after):
    rows_all, hidden = gg.shape
    experts = rows_all // (4 * cap)
    lhs = pl.BlockSpec((rows_all, hidden), lambda n, s: (0, 0))
    first = part * (columns // TILE)
    wide = pl.BlockSpec((None, TILE, hidden), lambda n, s: (0, s[h] + first + n, 0))
    out = pl.BlockSpec((2, experts * cap, TILE), lambda n, s: (0, 0, n))
    return pl.pallas_call(
        functools.partial(grad_kernel, cap, experts),
        out_shape=[jax.ShapeDtypeStruct((2, experts * cap, columns), jnp.bfloat16)] * 2,
        grid_spec=pltpu.PrefetchScalarGridSpec(
            num_scalar_prefetch=1,
            grid=(columns // TILE,),
            in_specs=[lhs, lhs, wide, wide] + [pl.BlockSpec(memory_space=pl.ANY)] * len(after),
            out_specs=[out, out],
        ),
        compiler_params=pltpu.CompilerParams(vmem_limit_bytes=50 * 2**20),
        cost_estimate=pl.CostEstimate(
            flops=4 * rows_all * hidden * columns,
            bytes_accessed=2 * (2 * rows_all * hidden + 2 * hidden * columns + rows_all * columns),
            transcendentals=0,
        ),
        name="grad",
    )(starts, gg, gu, w_gate, w_up, *after)


def planned(d_out, expert_ids, gate_weights, saved_gate, saved_up, w_gate, w_up, w_down, w_out):
    f32, bf16 = jnp.float32, jnp.bfloat16
    experts = lax.axis_size("expert")
    z, x, t = lax.axis_index("expert"), lax.axis_index("etp"), lax.axis_index("tp")
    y, c = t // 2, t % 2
    tokens, width = d_out.shape
    cap = saved_gate.shape[1] // (experts * 4)

    def over_z(v, shift):
        if shift % experts == 0:
            return v
        return lax.ppermute(v, "expert", [(i, (i + shift) % experts) for i in range(experts)])

    def over_x(v):
        return lax.ppermute(v, "etp", [(0, 1), (1, 0)])

    def over_y(v):
        return lax.ppermute(v, "tp", [(i, i ^ 2) for i in range(4)])

    def over_core(v):
        return lax.ppermute(v, "tp", [(i, i ^ 1) for i in range(4)])

    names = (z + jnp.arange(experts, dtype=jnp.int32)) % experts
    first_hit = expert_ids[:, 0:1] == names[None, :]
    second_hit = expert_ids[:, 1:2] == names[None, :]
    member = first_hit.astype(jnp.int32) + second_hit.astype(jnp.int32)
    weight = gate_weights[:, 0:1] * first_hit.astype(f32) + gate_weights[:, 1:2] * second_hit.astype(f32)
    slot = jnp.cumsum(member, axis=0) - member
    slot_iota = jnp.arange(cap, dtype=jnp.int32)
    select = (slot[:, :, None] == slot_iota[None, None, :]) & (member[:, :, None] > 0)
    slot_weight = jnp.sum(jnp.where(select, weight[:, :, None], 0.0), axis=0)
    select = select.astype(bf16)

    order = [0, 1] + list(range(experts - 1, 1, -1))
    arrived, near, groups = {}, {}, {}

    def fetch(k, after):
        packed = send_call(select[:, k].T, d_out, slot_weight[k][:, None], after)
        arrived[k] = over_z(packed, k)

    def spread(k):
        near[k] = over_x(arrived[k]), over_y(arrived[k])

    def finish(k, after):
        a, (bx, by) = arrived[k], near[k]
        corner = corner_call(bx, by, after)
        low, high = over_y(corner[0]), over_x(corner[1])
        groups[k] = (
            a, over_core(a), by, over_core(by),
            bx, over_core(bx), low, high, over_core(low), over_core(high),
        )

    for i, k in enumerate(order):
        fetch(k, () if i < 2 else (arrived[order[i - 1]],))
        spread(k)
    tiles = saved_gate.shape[2] // TILE
    grads = ()
    pairs = [order[i:i + 2] for i in range(0, experts, 2)]
    for k in pairs[0]:
        finish(k, ())
    for at, pair in enumerate(pairs):
        scalars = jnp.stack(
            [x * width, (1 - x) * width]
            + [(t ^ r) * cap for r in range(4)]
            + [(z - k) % experts for k in pair]
        ).astype(jnp.int32)
        later = pairs[at + 1] if at + 1 < len(pairs) else []
        cuts = (0, tiles // 2, tiles) if later else (0, tiles)
        for i in range(len(cuts) - 1):
            after = ()
            if later:
                after = (arrived[later[0]],) if i == 0 else (*near[later[0]], arrived[later[-1]])
            grads = act_call(
                at, cuts[i], cuts[i + 1] - cuts[i], scalars, [groups[k] for k in pair],
                w_down, saved_gate, saved_up, grads, after,
            )
            if later and i < len(later):
                finish(later[i], (grads[0],))
        for k in later:
            if k not in groups:
                finish(k, ())
    gg, gu = grads

    columns = width // COLUMN_PARTS
    starts = jnp.stack([x, 1 - x]).astype(jnp.int32) * (width // TILE)
    cut = experts // 2 * cap
    order = [k % experts for k in order]

    def add(*terms):
        return sum(v.astype(f32) for v in terms).astype(bf16)

    kept = {}
    summed, merged, owned, pieces, head_rows = {}, {}, {}, {}, []

    def stage_sum(h, part):
        keep, sent = kept[h, part]
        summed[h, part] = add(keep, sent)

    def stage_merge(part, after):
        merged[part] = merge_call(*kept[0, part], summed[1, part], *steps[part], after)

    def stage_own(part):
        to_x, to_y, base = merged[part]
        owned[part] = add(base, over_x(to_x), over_y(to_y))

    def stage_piece(part):
        own = owned[part]
        d_moe = 0.0
        for i, k in enumerate(order):
            back = over_z(own[i * cap:(i + 1) * cap], -k)
            d_moe = d_moe + jnp.dot(select[:, k], back, preferred_element_type=f32)
        here = d_out[:, part * columns:(part + 1) * columns].astype(f32)
        pieces[part] = (here + d_moe).astype(bf16)
        across = over_y(pieces[part])
        both = jnp.concatenate([pieces[part], across], axis=0)
        head_rows.append((both, over_core(both)))

    steps = {}
    for part in range(COLUMN_PARTS):
        for h in (1, 0):
            after = []
            if h == 1:
                if part >= 1:
                    stage_sum(1, part - 1)
                    s1 = summed[1, part - 1]
                    steps[part - 1] = over_x(s1[1, :cut]), over_y(s1[1, cut:])
                    after.append(s1)
                if part >= 2:
                    stage_own(part - 2)
                    after.append(owned[part - 2])
            else:
                if part >= 1:
                    stage_merge(part - 1, (kept[1, part][0],))
                    after += merged[part - 1][:2]
                if part >= 2:
                    stage_piece(part - 2)
                    after.append(pieces[part - 2])
            keep, sent = grad_call(h, part, columns, starts, gg, gu, w_gate, w_up, cap, after)
            kept[h, part] = keep, over_core(sent)
    end = COLUMN_PARTS - 1
    stage_sum(1, end)
    s1 = summed[1, end]
    steps[end] = over_x(s1[1, :cut]), over_y(s1[1, cut:])
    stage_merge(end, ())
    for part in range(max(end - 1, 0), COLUMN_PARTS):
        stage_own(part)
        stage_piece(part)
    hidden_parts = [pieces[part] for part in range(COLUMN_PARTS)]
    d_hidden = jnp.concatenate(hidden_parts, axis=1)
    own_core = jnp.concatenate([rows for rows, _ in head_rows], axis=1)
    other_core = jnp.concatenate([rows for _, rows in head_rows], axis=1)
    head = jnp.stack(
        [
            lax.dot_general(rows, w_out, NT, preferred_element_type=f32).astype(bf16)
            for rows in (own_core, other_core)
        ]
    ).reshape(2, 2, tokens, w_out.shape[0]).transpose(1, 0, 2, 3).reshape(2, 2 * tokens, -1)
    mine = jnp.where(y == x, head[0], head[1])
    theirs = jnp.where(y == x, head[1], head[0])
    total = (mine.astype(f32) + over_x(theirs).astype(f32)).astype(bf16)
    swapped = jnp.concatenate([total[tokens:], total[:tokens]], axis=0)
    return d_hidden, jnp.where(c == 0, total, swapped)


def general(d_out, expert_ids, gate_weights, saved_gate, saved_up, w_gate, w_up, w_down, w_out):
    expert_count = lax.axis_size("expert")
    tp_count = lax.axis_size("tp")
    feat_local = d_out.shape[1]
    cap_slots = saved_gate.shape[1] // (expert_count * tp_count)
    model_width = w_gate.shape[1]
    experts_iota = jnp.arange(expert_count, dtype=jnp.int32)
    first_hit = expert_ids[:, 0:1] == experts_iota[None, :]
    second_hit = expert_ids[:, 1:2] == experts_iota[None, :]
    member = first_hit.astype(jnp.int32) + second_hit.astype(jnp.int32)
    weight = gate_weights[:, 0:1] * first_hit.astype(jnp.float32) + gate_weights[
        :, 1:2
    ] * second_hit.astype(jnp.float32)
    slot = jnp.cumsum(member, axis=0) - member
    slot_iota = jnp.arange(cap_slots, dtype=jnp.int32)
    select = ((slot[:, :, None] == slot_iota[None, None, :]) & (member[:, :, None] > 0)).astype(
        jnp.float32
    )
    weighted_sel = select * weight[:, :, None]
    outgoing = jnp.einsum(
        "tec,td->ecd", weighted_sel, d_out.astype(jnp.float32), precision=lax.Precision.HIGHEST
    ).astype(jnp.bfloat16)
    received = lax.all_to_all(outgoing, "expert", split_axis=0, concat_axis=0, tiled=True)
    blocks_all = lax.all_gather(received[:, None], "tp", axis=1, tiled=True)
    down_local = w_down[0]
    slot_rows = blocks_all.shape[0] * blocks_all.shape[1] * blocks_all.shape[2]
    shard_piece = lax.all_gather(blocks_all, "etp", axis=3, tiled=True)
    width_piece = shard_piece.shape[3]
    flat_rows = shard_piece.reshape(slot_rows, width_piece)
    grad_act = lax.dot_general(
        flat_rows, down_local, (((1,), (1,)), ((), ())), preferred_element_type=jnp.float32
    )
    gate_val = saved_gate[0].astype(jnp.float32)
    up_val = saved_up[0].astype(jnp.float32)
    sigma = jax.nn.sigmoid(gate_val)
    grad_up = (grad_act * gate_val * sigma).astype(jnp.bfloat16)
    grad_gate = (grad_act * up_val * sigma * (1.0 + gate_val * (1.0 - sigma))).astype(jnp.bfloat16)
    gate_local = w_gate[0]
    up_local = w_up[0]
    first_part = lax.dot_general(
        gate_local, grad_gate, (((1,), (1,)), ((), ())), preferred_element_type=jnp.float32
    )
    whole_term = (
        first_part
        + lax.dot_general(
            up_local, grad_up, (((1,), (1,)), ((), ())), preferred_element_type=jnp.float32
        )
    ).reshape(model_width, expert_count, tp_count, cap_slots)
    by_block = lax.psum_scatter(
        whole_term.astype(jnp.bfloat16), "tp", scatter_dimension=2, tiled=True
    )
    reduced = lax.psum_scatter(by_block, "etp", scatter_dimension=0, tiled=True).astype(jnp.float32)
    returned = lax.all_to_all(
        reduced.reshape(feat_local, expert_count, cap_slots).astype(jnp.bfloat16),
        "expert",
        split_axis=1,
        concat_axis=1,
        tiled=True,
    ).astype(jnp.float32)
    d_moe = jnp.einsum("tec,dec->td", select, returned, precision=lax.Precision.HIGHEST)
    d_hidden = (d_out.astype(jnp.float32) + d_moe).astype(jnp.bfloat16)
    head_partial = lax.dot_general(
        lax.all_gather(d_hidden, "tp", axis=0, tiled=True),
        w_out,
        (((1,), (1,)), ((), ())),
        preferred_element_type=jnp.float32,
    )
    d_heads = lax.psum_scatter(
        head_partial.astype(jnp.bfloat16), "etp", scatter_dimension=0, tiled=True
    )
    return (d_hidden, d_heads)


def solution(mesh):
    pair_of_pairs = mesh.shape["etp"] == 2 and mesh.shape["tp"] == 4
    body = planned if pair_of_pairs else general
    in_specs = (
        P(("expert", "tp"), "etp"),
        P(("expert", "tp"), None),
        P(("expert", "tp"), None),
        P("expert", None, ("etp", "tp")),
        P("expert", None, ("etp", "tp")),
        P("expert", None, ("etp", "tp")),
        P("expert", None, ("etp", "tp")),
        P("expert", ("etp", "tp"), None),
        P("tp", "etp"),
    )
    out_specs = (P(("expert", "tp"), "etp"), P(("expert", "etp"), "tp"))
    return jax.shard_map(body, mesh=mesh, in_specs=in_specs, out_specs=out_specs, check_vma=False)
```

```python
import functools

import jax
import jax.numpy as jnp
from jax import lax
from jax.experimental import pallas as pl
from jax.experimental.pallas import tpu as pltpu
from jax.sharding import PartitionSpec as P

NT = (((1,), (1,)), ((), ()))
TILE = 256
COLUMN_PARTS = 4


def act_kernel(cap, width, groups, s_ref, *refs):
    blocks = refs[:10 * groups]
    wd = refs[10 * groups]
    saved = refs[10 * groups + 1:12 * groups + 1]
    gg, gu, lhs = refs[-3:]

    @pl.when(pl.program_id(0) == 0)
    def _():
        mine = pl.ds(pl.multiple_of(s_ref[0], 128), width)
        other = pl.ds(pl.multiple_of(s_ref[1], 128), width)
        half = cap // 2
        for j in range(groups):
            own0, own1, own2, own3, oth0, oth1, lo2, hi2, lo3, hi3 = blocks[10 * j:10 * j + 10]
            base = 4 * cap * j
            for r, block in enumerate((own0, own1, own2, own3)):
                lhs[base + r * cap:base + (r + 1) * cap, mine] = block[...]
            for r, block in enumerate((oth0, oth1)):
                lhs[base + r * cap:base + (r + 1) * cap, other] = block[...]
            for r, (low, high) in ((2, (lo2, hi2)), (3, (lo3, hi3))):
                lhs[base + r * cap:base + r * cap + half, other] = low[...]
                lhs[base + r * cap + half:base + (r + 1) * cap, other] = high[...]

    acc = lax.dot_general(lhs[...], wd[...], NT, preferred_element_type=jnp.float32)
    for j in range(groups):
        sg, su = saved[2 * j:2 * j + 2]
        for r in range(4):
            rows = pl.ds(pl.multiple_of(s_ref[2 + r], cap), cap)
            here = slice((4 * j + r) * cap, (4 * j + r + 1) * cap)
            g = sg[rows, :].astype(jnp.float32)
            u = su[rows, :].astype(jnp.float32)
            s = 1.0 / (1.0 + jnp.exp(-g))
            d = acc[here, :] * s
            gu[here, :] = (d * g).astype(jnp.bfloat16)
            gg[here, :] = (d * u * (1.0 + g * (1.0 - s))).astype(jnp.bfloat16)


def act_call(at, first, count, scalars, groups, w_down, saved_gate, saved_up, sofar, after):
    cap, width = groups[0][0].shape
    rows_all, hidden = saved_gate.shape[1:]
    model = w_down.shape[2]
    rows = 4 * cap * len(groups)
    blocks = [b for group in groups for b in group]
    full = [pl.BlockSpec(b.shape, lambda n, s: (0, 0)) for b in blocks]
    wide = pl.BlockSpec((None, TILE, model), lambda n, s: (0, first + n, 0))
    saved = []
    for j in range(len(groups)):
        saved += [pl.BlockSpec((None, 4 * cap, TILE), lambda n, s, j=j: (0, s[6 + j], first + n))] * 2
    held = [pl.BlockSpec(memory_space=pl.ANY)] * (len(sofar) + len(after))
    out = pl.BlockSpec((rows, TILE), lambda n, s: (at, first + n))
    ahead = 1 + len(blocks) + 1 + len(saved)
    return pl.pallas_call(
        functools.partial(act_kernel, cap, width, len(groups)),
        out_shape=[jax.ShapeDtypeStruct((rows_all, hidden), jnp.bfloat16)] * 2,
        grid_spec=pltpu.PrefetchScalarGridSpec(
            num_scalar_prefetch=1,
            grid=(count,),
            in_specs=full + [wide] + saved + held,
            out_specs=[out, out],
            scratch_shapes=[pltpu.VMEM((rows, model), jnp.bfloat16)],
        ),
        input_output_aliases={ahead + i: i for i in range(len(sofar))},
        compiler_params=pltpu.CompilerParams(vmem_limit_bytes=50 * 2**20),
        cost_estimate=pl.CostEstimate(
            flops=2 * rows * model * count * TILE,
            bytes_accessed=2 * (count * TILE * model + rows * model + 4 * rows * count * TILE),
            transcendentals=rows * count * TILE,
        ),
        name="act",
    )(scalars, *blocks, w_down, *([saved_gate, saved_up] * len(groups)), *sofar, *after)


def grad_kernel(cap, experts, s_ref, gg, gu, wg, wu, *refs):
    keep, send = refs[-2:]
    res = lax.dot_general(gg[...], wg[...], NT, preferred_element_type=jnp.float32)
    res += lax.dot_general(gu[...], wu[...], NT, preferred_element_type=jnp.float32)
    res = res.astype(jnp.bfloat16)
    for k in range(experts):
        for v in range(2):
            at = (4 * k + 2 * v) * cap
            keep[v, k * cap:(k + 1) * cap, :] = res[at:at + cap]
            send[v, k * cap:(k + 1) * cap, :] = res[at + cap:at + 2 * cap]


def grad_call(part, columns, starts, gg, gu, w_gate, w_up, cap, after):
    rows_all, hidden = gg.shape
    experts = rows_all // (4 * cap)
    lhs = pl.BlockSpec((rows_all, hidden), lambda h, n, s: (0, 0))
    first = part * (columns // TILE)
    wide = pl.BlockSpec((None, TILE, hidden), lambda h, n, s: (0, s[h] + first + n, 0))
    out = pl.BlockSpec((None, 2, experts * cap, TILE), lambda h, n, s: (h, 0, 0, n))
    return pl.pallas_call(
        functools.partial(grad_kernel, cap, experts),
        out_shape=[jax.ShapeDtypeStruct((2, 2, experts * cap, columns), jnp.bfloat16)] * 2,
        grid_spec=pltpu.PrefetchScalarGridSpec(
            num_scalar_prefetch=1,
            grid=(2, columns // TILE),
            in_specs=[lhs, lhs, wide, wide] + [pl.BlockSpec(memory_space=pl.ANY)] * len(after),
            out_specs=[out, out],
        ),
        compiler_params=pltpu.CompilerParams(vmem_limit_bytes=50 * 2**20),
        cost_estimate=pl.CostEstimate(
            flops=8 * rows_all * hidden * columns,
            bytes_accessed=2 * (2 * rows_all * hidden + 4 * hidden * columns + 2 * rows_all * columns),
            transcendentals=0,
        ),
        name="grad",
    )(starts, gg, gu, w_gate, w_up, *after)


def planned(d_out, expert_ids, gate_weights, saved_gate, saved_up, w_gate, w_up, w_down, w_out):
    f32, bf16 = jnp.float32, jnp.bfloat16
    experts = lax.axis_size("expert")
    z, x, t = lax.axis_index("expert"), lax.axis_index("etp"), lax.axis_index("tp")
    y, c = t // 2, t % 2
    tokens, width = d_out.shape
    cap = saved_gate.shape[1] // (experts * 4)

    def over_z(v, shift):
        if shift % experts == 0:
            return v
        return lax.ppermute(v, "expert", [(i, (i + shift) % experts) for i in range(experts)])

    def over_x(v):
        return lax.ppermute(v, "etp", [(0, 1), (1, 0)])

    def over_y(v):
        return lax.ppermute(v, "tp", [(i, i ^ 2) for i in range(4)])

    def over_core(v):
        return lax.ppermute(v, "tp", [(i, i ^ 1) for i in range(4)])

    names = (z + jnp.arange(experts, dtype=jnp.int32)) % experts
    first_hit = expert_ids[:, 0:1] == names[None, :]
    second_hit = expert_ids[:, 1:2] == names[None, :]
    member = first_hit.astype(jnp.int32) + second_hit.astype(jnp.int32)
    weight = gate_weights[:, 0:1] * first_hit.astype(f32) + gate_weights[:, 1:2] * second_hit.astype(f32)
    slot = jnp.cumsum(member, axis=0) - member
    slot_iota = jnp.arange(cap, dtype=jnp.int32)
    select = (slot[:, :, None] == slot_iota[None, None, :]) & (member[:, :, None] > 0)
    slot_weight = jnp.sum(jnp.where(select, weight[:, :, None], 0.0), axis=0)
    select = select.astype(bf16)

    gathered = []
    for k in range(experts):
        rows = lax.dot_general(
            select[:, k], d_out, (((0,), (0,)), ((), ())), preferred_element_type=f32
        )
        gathered.append(over_z((rows * slot_weight[k][:, None]).astype(bf16), k))

    groups = []
    half = cap // 2
    for k in range(experts):
        a = gathered[k]
        bx, by = over_x(a), over_y(a)
        low, high = over_y(bx[:half]), over_x(by[half:])
        groups.append((
            a, over_core(a), by, over_core(by),
            bx, over_core(bx), low, high, over_core(low), over_core(high),
        ))
    grads = ()
    for at in range(experts // 2):
        pair = (2 * at, 2 * at + 1)
        scalars = jnp.stack(
            [x * width, (1 - x) * width]
            + [(t ^ r) * cap for r in range(4)]
            + [(z - k) % experts for k in pair]
        ).astype(jnp.int32)
        grads = act_call(
            at, 0, saved_gate.shape[2] // TILE, scalars, [groups[k] for k in pair],
            w_down, saved_gate, saved_up, grads, (),
        )
    gg, gu = grads

    columns = width // COLUMN_PARTS
    starts = jnp.stack([x, 1 - x]).astype(jnp.int32) * (width // TILE)
    cut = experts // 2 * cap
    hidden_parts, head_rows = [], []
    sums, outgoing = [], []
    for part in range(COLUMN_PARTS):
        after = sums[part - 2:part - 1] if part >= 2 else []
        if part >= 3:
            after = [*after, *outgoing[part - 3]]
        keep, send = grad_call(part, columns, starts, gg, gu, w_gate, w_up, cap, after)
        both = (keep.astype(f32) + over_core(send).astype(f32)).astype(bf16)
        sums.append(both)
        via_x, via_y = over_x(both[1, 1, :cut]), over_y(both[1, 1, cut:])
        to_y = jnp.concatenate(
            [(both[0, 1, :cut].astype(f32) + via_x.astype(f32)).astype(bf16), both[0, 1, cut:]]
        )
        to_x = jnp.concatenate(
            [both[1, 0, :cut], (both[1, 0, cut:].astype(f32) + via_y.astype(f32)).astype(bf16)]
        )
        outgoing.append((to_x, to_y))
        from_x, from_y = over_x(to_x), over_y(to_y)
        own = (both[0, 0].astype(f32) + from_x.astype(f32) + from_y.astype(f32)).astype(bf16)
        back = [over_z(own[k * cap:(k + 1) * cap], -k) for k in range(experts)]
        d_moe = 0.0
        for k in range(experts):
            d_moe = d_moe + jnp.dot(select[:, k], back[k], preferred_element_type=f32)
        here = d_out[:, part * columns:(part + 1) * columns].astype(f32)
        piece = (here + d_moe).astype(bf16)
        hidden_parts.append(piece)
        across = over_y(piece)
        head_rows.append(
            jnp.concatenate([piece, over_core(piece), across, over_core(across)], axis=0)
        )
    d_hidden = jnp.concatenate(hidden_parts, axis=1)
    head = 0.0
    for part in range(COLUMN_PARTS):
        head = head + lax.dot_general(
            head_rows[part],
            w_out[:, part * columns:(part + 1) * columns],
            NT,
            preferred_element_type=f32,
        )
    head = head.astype(bf16).reshape(2, 2 * tokens, w_out.shape[0])
    mine = jnp.where(y == x, head[0], head[1])
    theirs = jnp.where(y == x, head[1], head[0])
    total = (mine.astype(f32) + over_x(theirs).astype(f32)).astype(bf16)
    swapped = jnp.concatenate([total[tokens:], total[:tokens]], axis=0)
    return d_hidden, jnp.where(c == 0, total, swapped)


def general(d_out, expert_ids, gate_weights, saved_gate, saved_up, w_gate, w_up, w_down, w_out):
    expert_count = lax.axis_size("expert")
    tp_count = lax.axis_size("tp")
    feat_local = d_out.shape[1]
    cap_slots = saved_gate.shape[1] // (expert_count * tp_count)
    model_width = w_gate.shape[1]
    experts_iota = jnp.arange(expert_count, dtype=jnp.int32)
    first_hit = expert_ids[:, 0:1] == experts_iota[None, :]
    second_hit = expert_ids[:, 1:2] == experts_iota[None, :]
    member = first_hit.astype(jnp.int32) + second_hit.astype(jnp.int32)
    weight = gate_weights[:, 0:1] * first_hit.astype(jnp.float32) + gate_weights[
        :, 1:2
    ] * second_hit.astype(jnp.float32)
    slot = jnp.cumsum(member, axis=0) - member
    slot_iota = jnp.arange(cap_slots, dtype=jnp.int32)
    select = ((slot[:, :, None] == slot_iota[None, None, :]) & (member[:, :, None] > 0)).astype(
        jnp.float32
    )
    weighted_sel = select * weight[:, :, None]
    outgoing = jnp.einsum(
        "tec,td->ecd", weighted_sel, d_out.astype(jnp.float32), precision=lax.Precision.HIGHEST
    ).astype(jnp.bfloat16)
    received = lax.all_to_all(outgoing, "expert", split_axis=0, concat_axis=0, tiled=True)
    blocks_all = lax.all_gather(received[:, None], "tp", axis=1, tiled=True)
    down_local = w_down[0]
    slot_rows = blocks_all.shape[0] * blocks_all.shape[1] * blocks_all.shape[2]
    shard_piece = lax.all_gather(blocks_all, "etp", axis=3, tiled=True)
    width_piece = shard_piece.shape[3]
    flat_rows = shard_piece.reshape(slot_rows, width_piece)
    grad_act = lax.dot_general(
        flat_rows, down_local, (((1,), (1,)), ((), ())), preferred_element_type=jnp.float32
    )
    gate_val = saved_gate[0].astype(jnp.float32)
    up_val = saved_up[0].astype(jnp.float32)
    sigma = jax.nn.sigmoid(gate_val)
    grad_up = (grad_act * gate_val * sigma).astype(jnp.bfloat16)
    grad_gate = (grad_act * up_val * sigma * (1.0 + gate_val * (1.0 - sigma))).astype(jnp.bfloat16)
    gate_local = w_gate[0]
    up_local = w_up[0]
    first_part = lax.dot_general(
        gate_local, grad_gate, (((1,), (1,)), ((), ())), preferred_element_type=jnp.float32
    )
    whole_term = (
        first_part
        + lax.dot_general(
            up_local, grad_up, (((1,), (1,)), ((), ())), preferred_element_type=jnp.float32
        )
    ).reshape(model_width, expert_count, tp_count, cap_slots)
    by_block = lax.psum_scatter(
        whole_term.astype(jnp.bfloat16), "tp", scatter_dimension=2, tiled=True
    )
    reduced = lax.psum_scatter(by_block, "etp", scatter_dimension=0, tiled=True).astype(jnp.float32)
    returned = lax.all_to_all(
        reduced.reshape(feat_local, expert_count, cap_slots).astype(jnp.bfloat16),
        "expert",
        split_axis=1,
        concat_axis=1,
        tiled=True,
    ).astype(jnp.float32)
    d_moe = jnp.einsum("tec,dec->td", select, returned, precision=lax.Precision.HIGHEST)
    d_hidden = (d_out.astype(jnp.float32) + d_moe).astype(jnp.bfloat16)
    head_partial = lax.dot_general(
        lax.all_gather(d_hidden, "tp", axis=0, tiled=True),
        w_out,
        (((1,), (1,)), ((), ())),
        preferred_element_type=jnp.float32,
    )
    d_heads = lax.psum_scatter(
        head_partial.astype(jnp.bfloat16), "etp", scatter_dimension=0, tiled=True
    )
    return (d_hidden, d_heads)


def solution(mesh):
    pair_of_pairs = mesh.shape["etp"] == 2 and mesh.shape["tp"] == 4
    body = planned if pair_of_pairs else general
    in_specs = (
        P(("expert", "tp"), "etp"),
        P(("expert", "tp"), None),
        P(("expert", "tp"), None),
        P("expert", None, ("etp", "tp")),
        P("expert", None, ("etp", "tp")),
        P("expert", None, ("etp", "tp")),
        P("expert", None, ("etp", "tp")),
        P("expert", ("etp", "tp"), None),
        P("tp", "etp"),
    )
    out_specs = (P(("expert", "tp"), "etp"), P(("expert", "etp"), "tp"))
    return jax.shard_map(body, mesh=mesh, in_specs=in_specs, out_specs=out_specs, check_vma=False)
```
